256 devices in a mesh: expert: 64 (over z, x, y_hi), replica: 4 (over y_lo, core).
Axes of the slice: x: 4, y: 4 (y_hi: 2, y_lo: 2; y = y_hi * 2 + y_lo), z: 8, core: 2. Of those that a mesh axis runs over, the one named last changes fastest.
Arguments:
- tokens: bfloat16 [32768, 1024], P(('expert', 'replica')), may hold values from -6 to 6
- upstream: bfloat16 [32768, 1024], P(('expert', 'replica')), may hold values from -2 to 2
- expert_ids: int32 [32768, 2], P(('expert', 'replica')), may hold values from 0 to 63, as said below
- slot_index: int32 [32768, 2], P(('expert', 'replica')), may hold values from -1 to 4, as said below
- gate_weights: float32 [32768, 2], P(('expert', 'replica')), may hold values from 0.2 to 1
- in_weight: bfloat16 [64, 1024, 4096], P('expert', None, 'replica'), may hold values from -0.1875 to 0.1875
- out_weight: bfloat16 [64, 4096, 1024], P('expert', 'replica'), may hold values from -0.09375 to 0.09375
Outputs:
- token_grad: bfloat16 [32768, 1024], P(('expert', 'replica'))
- grad_in: bfloat16 [64, 1024, 4096], P('expert', None, 'replica')
- grad_out: bfloat16 [64, 4096, 1024], P('expert', 'replica')
The draws below stay inside these ranges and needn't reach their ends.
Inputs may be any that keep to these rules, and one draw needn't show every extreme that they name: `expert_ids`: each token names two different experts. `slot_index`: the number of earlier assignments of the same group to the same expert, counted in token order then in column order, or -1 where that number is 5 or more; in every group some expert has all 5 slots filled.
All inputs are finite; a program needn't handle non-finite values.
Results may differ from the reference program's by a relative error of at most 0.014.
Values may be sent and summed in bfloat16 or wider, within the bound.
No kernel may reach another device: no remote copies, remote signals or barrier semaphores. Data moves between devices by JAX's collectives and lax.ppermute only.
A program may use at most 128 MiB of HBM per device.

```python
import jax
import jax.numpy as jnp
from jax import lax

D = 1024
FF = 4096
TOK_DEV = 128
CAP = 5
EXPERTS = 64
TOKENS = 32768
N_EXPERT = 64
N_REPLICA = 4


def routing(key):
    order_key, low_key, high_key, offset_key, forced_key = jax.random.split(key, 5)
    expert_order = jax.random.permutation(order_key, EXPERTS)
    lower_draw = jnp.minimum(jax.random.randint(low_key, (TOKENS,), 0, EXPERTS), jax.random.randint(high_key, (TOKENS,), 0, EXPERTS))
    primary = expert_order[lower_draw]
    forced_expert = jax.random.randint(forced_key, (), 0, EXPERTS)
    position_in = jnp.arange(TOKENS) % TOK_DEV
    primary = jnp.where(position_in <= CAP, forced_expert, primary)
    offset_draw = jax.random.randint(offset_key, (TOKENS,), 1, EXPERTS)
    secondary = (primary + offset_draw) % EXPERTS
    chosen = jnp.stack([primary, secondary], axis=1).astype(jnp.int32)
    block_count = TOKENS // TOK_DEV
    flat_ids = chosen.reshape(block_count, 2 * TOK_DEV)
    one_hot = (flat_ids[:, :, None] == jnp.arange(EXPERTS)[None, None, :]).astype(jnp.int32)
    before = jnp.cumsum(one_hot, axis=1) - one_hot
    counted = jnp.sum(before * one_hot, axis=2).reshape(TOKENS, 2)
    slot_value = jnp.where(counted < CAP, counted, -1).astype(jnp.int32)
    return (chosen, slot_value)


def draw_expert_ids(key, part):
    chosen, slot_value = routing(key)
    return chosen


def draw_slot_index(key, part):
    chosen, slot_value = routing(key)
    return slot_value


def block_levels(key, extent, shards, low, high):
    def one(position, shards_of):
        steps = jax.random.uniform(jax.random.fold_in(jax.random.fold_in(key, 6), position), (shards_of,), jnp.float32, low / len(shards), high / len(shards))
        return jnp.repeat(jnp.exp(steps), extent[position] // shards_of).reshape((-1,) + (1,) * (len(extent) - position - 1))

    factor_of = one(*shards[0])
    for cut in shards[1:]:
        factor_of = factor_of * one(*cut)
    return factor_of


def gaussian(own_key, shape, scale, limit, pieces=(), dtype=jnp.bfloat16):
    array = jax.random.normal(own_key, shape, jnp.float32) * scale
    if len(pieces) > 0:
        array = block_levels(own_key, shape, pieces, -0.22, 0.18) * array
    return jnp.clip(array, min=-limit, max=limit).astype(dtype)


def setup_inputs(seed: int = 0) -> dict:
    splits = jax.random.split(jax.random.key(seed), 8)
    tokens = gaussian(splits[0], (TOKENS, D), 1.0, 6.0, ((0, 256),))
    upstream = gaussian(splits[1], (TOKENS, D), 0.3, 2.0, ((0, 256),))
    expert_ids = draw_expert_ids(jax.random.fold_in(splits[7], 71), 0)
    slot_index = draw_slot_index(jax.random.fold_in(splits[7], 71), 0)
    gate_weights = jnp.clip(0.2 + 0.8 * jax.random.uniform(splits[4], (TOKENS, 2), jnp.float32) ** block_levels(splits[4], (TOKENS, 2), ((0, 256),), -0.2, 0.2), 0.2, 1.0)
    in_weight = gaussian(splits[5], (EXPERTS, D, FF), D ** -0.5, 0.1875, ((0, 64), (2, 4)))
    out_weight = gaussian(splits[6], (EXPERTS, FF, D), FF ** -0.5, 0.09375, ((0, 64), (1, 4)))
    return dict(tokens=tokens, upstream=upstream, expert_ids=expert_ids, slot_index=slot_index, gate_weights=gate_weights, in_weight=in_weight, out_weight=out_weight)


def smooth_gate(value):
    return jax.nn.gelu(value, approximate=True)

def hidden_step(input_rows, grad_rows, weight_in, weight_out):
    hidden = jnp.dot(input_rows, weight_in, preferred_element_type=jnp.float32)
    active, pullback = jax.vjp(smooth_gate, hidden)
    carried = lax.dot_general(grad_rows, weight_out, (((1,), (1,)), ((), ())), preferred_element_type=jnp.float32)
    grad_hidden = pullback(carried)[0].astype(jnp.bfloat16)
    return (active.astype(jnp.bfloat16), grad_hidden)

def replica_sums(first_factor, second_factor, groups):
    row_count = first_factor.shape[0] // groups
    summands = jnp.einsum('grf,grd->gfd', first_factor.reshape(groups, row_count, -1).astype(jnp.float32), second_factor.reshape(groups, row_count, -1).astype(jnp.float32))
    rounded = lax.optimization_barrier(summands.astype(jnp.bfloat16))
    return lax.optimization_barrier(jnp.sum(rounded.astype(jnp.float32), axis=0))

def reference(tokens, upstream, expert_ids, slot_index, gate_weights, in_weight, out_weight):
    per_expert = N_REPLICA * N_EXPERT * CAP
    total = EXPERTS * per_expert
    grid_shape = (N_EXPERT, N_REPLICA, TOK_DEV, 2)
    chosen = expert_ids.reshape(grid_shape)
    slot_value = slot_index.reshape(grid_shape)
    source = lax.broadcasted_iota(jnp.int32, grid_shape, 0)
    replica = lax.broadcasted_iota(jnp.int32, grid_shape, 1)
    target = ((chosen * N_REPLICA + replica) * N_EXPERT + source) * CAP + slot_value
    target = jnp.where(slot_value >= 0, target, total).reshape(-1).astype(jnp.int32)
    spread_tokens = jnp.broadcast_to(tokens.reshape(N_EXPERT, N_REPLICA, TOK_DEV, 1, D), grid_shape + (D,)).reshape(-1, D)
    expert_rows = jnp.zeros((total + 1, D), jnp.bfloat16).at[target].set(spread_tokens)[:total].reshape(EXPERTS, per_expert, D)
    scaled = gate_weights.reshape(grid_shape)[..., None] * upstream.reshape(N_EXPERT, N_REPLICA, TOK_DEV, 1, D).astype(jnp.float32)
    expert_grads = jnp.zeros((total + 1, D), jnp.float32).at[target].add(scaled.reshape(-1, D))[:total]
    expert_grads = expert_grads.astype(jnp.bfloat16).reshape(EXPERTS, per_expert, D)

    def one_expert(items):
        input_rows, grad_rows, weight_in, weight_out = items
        active, grad_hidden = hidden_step(input_rows, grad_rows, weight_in, weight_out)
        returned = lax.dot_general(grad_hidden, weight_in, (((1,), (1,)), ((), ())), preferred_element_type=jnp.float32).astype(jnp.bfloat16)
        grad_output = replica_sums(active, grad_rows, N_REPLICA).astype(jnp.bfloat16)
        grad_input = replica_sums(grad_hidden, input_rows, N_REPLICA).T.astype(jnp.bfloat16)
        return (returned, grad_input, grad_output)
    returned, grad_in, grad_out = lax.map(one_expert, (expert_rows, expert_grads, in_weight, out_weight))
    flat_rows = jnp.concatenate([returned.reshape(total, D), jnp.zeros((1, D), jnp.bfloat16)], axis=0)
    picked = flat_rows[target].reshape(N_EXPERT, N_REPLICA, TOK_DEV, 2, D).astype(jnp.float32)
    token_grad = lax.optimization_barrier(jnp.sum(picked, axis=3)).astype(jnp.bfloat16).reshape(TOKENS, D)
    return (token_grad, grad_in, grad_out)
```

```python
import jax
import jax.numpy as jnp
from jax import lax
from jax.sharding import PartitionSpec as P

BF = jnp.bfloat16
F32 = jnp.float32
LANES = 128
TO_CORE = ((0, 1), (1, 0), (2, 3), (3, 2))
TO_CHIP = ((0, 2), (2, 0), (1, 3), (3, 1))


def smooth_gate(value):
    return jax.nn.gelu(value, approximate=True)


def dot(a, b, dims):
    return lax.dot_general(a, b, ((dims[0], dims[1]), ((), ())), preferred_element_type=F32)


def exchange(rows, experts):
    count, width = rows.shape
    blocks = rows.reshape(experts, count // experts * (width // LANES), LANES)
    moved = lax.all_to_all(blocks, "expert", split_axis=0, concat_axis=0, tiled=True)
    return moved.reshape(count, width)


def to_core(rows):
    return lax.ppermute(rows, "replica", TO_CORE)


def to_chip(rows):
    return lax.ppermute(rows, "replica", TO_CHIP)


def shards(tokens, upstream, expert_ids, slot_index, gate_weights, in_weight, out_weight):
    token_count, width = tokens.shape
    experts = lax.axis_size("expert")
    capacity = 5 * token_count // (2 * experts)
    columns = experts * capacity
    target = jnp.where(slot_index >= 0, expert_ids * capacity + slot_index, -1)
    column_ids = lax.broadcasted_iota(jnp.int32, (columns, 1), 0)
    first = column_ids == target[:, 0][None, :]
    second = column_ids == target[:, 1][None, :]
    place = (first | second).astype(BF)
    gates = jnp.where(first, gate_weights[:, 0][None, :], 0.0) + jnp.where(
        second, gate_weights[:, 1][None, :], 0.0
    )
    slot_gate = jnp.sum(gates, axis=1, keepdims=True)
    sent_tokens = dot(place, tokens, ((1,), (0,))).astype(BF)
    sent_grads = (slot_gate * dot(place, upstream, ((1,), (0,)))).astype(BF)
    if COMBINED:
        per = capacity * (width // LANES)
        both = jnp.concatenate([sent_tokens.reshape(experts, per, LANES), sent_grads.reshape(experts, per, LANES)], axis=1)
        both = lax.all_to_all(both, "expert", split_axis=0, concat_axis=0, tiled=True)
        x_own = both[:, :per].reshape(columns, width)
        g_own = both[:, per:].reshape(columns, width)
    else:
        x_own = exchange(sent_tokens, experts)
        g_own = exchange(sent_grads, experts)
    w_in = in_weight[0]
    w_out = out_weight[0]
    x_chip = to_chip(x_own)
    g_chip = to_chip(g_own)
    x_core = to_core(x_own)
    g_core = to_core(g_own)
    x_far = to_core(x_chip)
    g_far = to_core(g_chip)
    x_all = jnp.concatenate([x_own, x_core, x_chip, x_far], axis=0)
    g_all = jnp.concatenate([g_own, g_core, g_chip, g_far], axis=0)
    hidden = dot(x_all, w_in, ((1,), (0,)))
    active, pullback = jax.vjp(smooth_gate, hidden)
    carried = dot(g_all, w_out, ((1,), (1,)))
    grad_hidden = pullback(carried)[0].astype(BF)
    active = active.astype(BF)
    partial = dot(grad_hidden, w_in, ((1,), (1,)))
    n = columns
    away = jnp.concatenate([partial[n : 2 * n], partial[3 * n :]], axis=0).astype(BF)
    back = to_core(away)
    own = partial[:n] + back[:n].astype(F32)
    chip = (partial[2 * n : 3 * n] + back[n:].astype(F32)).astype(BF)
    returned = (own + to_chip(chip).astype(F32)).astype(BF)
    grad_out = dot(active, g_all, ((0,), (0,))).astype(BF)
    grad_in = dot(x_all, grad_hidden, ((0,), (0,))).astype(BF)
    arrived = exchange(returned, experts)
    token_grad = dot(place, arrived, ((0,), (0,))).astype(BF)
    return token_grad, grad_in[None], grad_out[None]


COMBINED = True


def solution(mesh):
    rows = P(("expert", "replica"), None)
    return jax.shard_map(
        shards,
        mesh=mesh,
        in_specs=(rows, rows, rows, rows, rows, P("expert", None, "replica"), P("expert", "replica", None)),
        out_specs=(rows, P("expert", None, "replica"), P("expert", "replica", None)),
        check_vma=False,
    )
```

```python
import functools

import jax
import jax.numpy as jnp
from jax import lax
from jax.experimental import pallas as pl
from jax.experimental.pallas import tpu as pltpu
from jax.sharding import PartitionSpec as P

BF = jnp.bfloat16
F32 = jnp.float32
LANES = 128
SCALE = 0.7978845608
CUBE = 0.044715
TO_CORE = ((0, 1), (1, 0), (2, 3), (3, 2))
TO_CHIP = ((0, 2), (2, 0), (1, 3), (3, 1))
SPLIT = (32, 32)
SMALL = 16 * 2**20
LARGE = 56 * 2**20


def dot(a, b, dims):
    return lax.dot_general(a, b, ((dims[0], dims[1]), ((), ())), preferred_element_type=F32)


def kernel_call(body, out_shape, limit, flops, size, **kw):
    return pl.pallas_call(
        body,
        out_shape=out_shape,
        compiler_params=pltpu.CompilerParams(vmem_limit_bytes=limit),
        cost_estimate=pl.CostEstimate(flops=flops, bytes_accessed=size, transcendentals=0),
        **kw,
    )


def shape(rows, width, dtype=BF):
    return jax.ShapeDtypeStruct((rows, width), dtype)


def to_core(rows):
    return lax.ppermute(rows, "replica", TO_CORE)


def to_chip(rows):
    return lax.ppermute(rows, "replica", TO_CHIP)


def places(ids, slots, capacity, columns):
    target = jnp.where(slots >= 0, ids * capacity + slots, -1)
    column_ids = lax.broadcasted_iota(jnp.int32, (columns, target.shape[1]), 0)
    return column_ids == target[0:1, :], column_ids == target[1:2, :]


def pack(rows, experts):
    count, width = rows.shape
    return rows.reshape(count, width // LANES, LANES).reshape(experts, -1, LANES)


def dispatch_kernel(experts, capacity, tokens, upstream, ids, slots, gates, sent):
    columns = experts * capacity
    first, second = places(ids[...], slots[...], capacity, columns)
    place = jnp.where(first | second, 1.0, 0.0).astype(BF)
    gate = jnp.where(first, gates[0:1, :], 0.0) + jnp.where(second, gates[1:2, :], 0.0)
    slot_gate = jnp.sum(gate, axis=1, keepdims=True)
    rows = dot(place, tokens[...], ((1,), (0,)))
    grads = slot_gate * dot(place, upstream[...], ((1,), (0,)))
    both = jnp.concatenate([pack(rows, experts), pack(grads, experts)], axis=1)
    sent[...] = both.reshape(-1, LANES).astype(BF)


def unpack_kernel(senders, got, own):
    blocks = got[...].astype(F32).reshape(senders, -1, LANES)
    per = blocks.shape[1] // 2
    n = own.shape[0] // 2
    own[pl.ds(0, n), :] = blocks[:, :per].reshape(n, -1).astype(BF)
    own[pl.ds(n, n), :] = blocks[:, per:].reshape(n, -1).astype(BF)


def expert_kernel(sizes, *refs):
    blocks, refs = refs[: len(sizes)], refs[len(sizes) :]
    w_in, w_out, active, grad_hidden, away, near = refs
    split = away.shape[0]
    x = jnp.concatenate([block[pl.ds(0, n), :] for n, block in zip(sizes, blocks)], axis=0)
    g = jnp.concatenate([block[pl.ds(n, n), :] for n, block in zip(sizes, blocks)], axis=0)
    hidden = dot(x, w_in[...], ((1,), (0,)))
    carried = dot(g, w_out[...], ((1,), (1,)))
    square = hidden * hidden
    bend = jnp.tanh(hidden * (SCALE + SCALE * CUBE * square))
    lift = 0.5 * (1.0 + bend)
    active[...] = (hidden * lift).astype(BF)
    slope = lift + hidden * (1.0 - bend * bend) * (0.5 * SCALE + 1.5 * SCALE * CUBE * square)
    back = (slope * carried).astype(BF)
    grad_hidden[...] = back
    part = dot(back, w_in[...], ((1,), (1,)))
    away[...] = part[:split].astype(BF)
    near[...] = part[split:]


def expert_step(blocks, w_in, w_out):
    width, units = w_in.shape
    sizes = [block.shape[0] // 2 for block in blocks]
    rows = sum(sizes)
    return kernel_call(
        functools.partial(expert_kernel, sizes),
        [shape(rows, units), shape(rows, units), shape(rows // 2, width), shape(rows // 2, width, F32)],
        LARGE,
        6 * rows * width * units,
        4 * width * units + 14 * rows * width,
    )(*blocks, w_in, w_out)


def weight_grads_kernel(sizes, runs, *refs):
    blocks, refs = refs[: len(sizes)], refs[len(sizes) :]
    count = len(runs)
    actives, refs = refs[:count], refs[count:]
    grad_hiddens, (grad_in, grad_out) = refs[:count], refs[count:]
    out_sum = in_sum = None
    at = 0
    for active, grad_hidden, run in zip(actives, grad_hiddens, runs):
        sides = list(zip(sizes[at : at + run], blocks[at : at + run]))
        at += run
        x = jnp.concatenate([block[pl.ds(0, n), :] for n, block in sides], axis=0)
        g = jnp.concatenate([block[pl.ds(n, n), :] for n, block in sides], axis=0)
        out_part = dot(active[...], g, ((0,), (0,)))
        in_part = dot(grad_hidden[...], x, ((0,), (0,)))
        out_sum = out_part if out_sum is None else out_sum + out_part
        in_sum = in_part if in_sum is None else in_sum + in_part
    grad_out[...] = out_sum.astype(BF)
    grad_in[...] = in_sum.T.astype(BF)


def weight_grads(made, width, units):
    tile = 256
    blocks = [block for group, _, _ in made for block in group]
    sizes = [block.shape[0] // 2 for block in blocks]
    runs = [len(group) for group, _, _ in made]
    rows = [active.shape[0] for _, active, _ in made]
    columns = [pl.BlockSpec((n, tile), lambda j: (0, j)) for n in rows]
    return kernel_call(
        functools.partial(weight_grads_kernel, sizes, runs),
        [shape(width, units), shape(units, width)],
        LARGE,
        4 * sum(rows) * width * units,
        4 * width * units + 8 * sum(rows) * width,
        grid=(units // tile,),
        in_specs=[pl.BlockSpec((2 * n, width), lambda j: (0, 0)) for n in sizes] + columns + columns,
        out_specs=[pl.BlockSpec((width, tile), lambda j: (0, j)), pl.BlockSpec((tile, width), lambda j: (j, 0))],
    )(*blocks, *[m[1] for m in made], *[m[2] for m in made])


def return_kernel(capacity, near, back, *refs):
    chips, out = refs[:-1], refs[-1]
    start = 0
    packed = []
    for chip in chips:
        n = chip.shape[0]
        at = pl.ds(start, n)
        rows = near[at, :] + back[at, :].astype(F32) + chip[...].astype(F32)
        packed.append(pack(rows, n // capacity).reshape(-1, LANES))
        start += n
    out[...] = jnp.concatenate(packed, axis=0).astype(BF)


def exchange(blocks, experts):
    moved = lax.all_to_all(blocks.reshape(experts, -1, LANES), "expert", split_axis=0, concat_axis=0, tiled=True)
    return moved.reshape(-1, LANES)


def reduce_core(away, near):
    return to_chip((near + to_core(away).astype(F32)).astype(BF))


def shards(tokens, upstream, expert_ids, slot_index, gate_weights, in_weight, out_weight):
    token_count, width = tokens.shape
    experts = lax.axis_size("expert")
    capacity = 5 * token_count // (2 * experts)
    columns = experts * capacity
    per = width // LANES * capacity * 2
    ids, slots, gates = expert_ids.T, slot_index.T, gate_weights.T
    sent = kernel_call(
        functools.partial(dispatch_kernel, experts, capacity), shape(experts * per, LANES), LARGE, 1, 1
    )(tokens, upstream, ids, slots, gates)
    got = exchange(sent, experts)
    w_in = in_weight[0]
    w_out = out_weight[0]
    owns = []
    start = 0
    for senders in SPLIT:
        at = start // senders
        owns.append(
            kernel_call(
                functools.partial(unpack_kernel, senders),
                shape(2 * senders * capacity, width),
                SMALL,
                10**6,
                10**6,
                grid=(1,),
                in_specs=[pl.BlockSpec((senders * per, LANES), lambda j, at=at: (at, 0))],
                out_specs=pl.BlockSpec((2 * senders * capacity, width), lambda j: (0, 0)),
            )(got)
        )
        start += senders
    barrier = lax.optimization_barrier
    cores = [to_core(own) for own in owns]
    blocks = cores + owns
    active, grad_hidden, away_own, near_own = expert_step(blocks, w_in, w_out)
    back_own = to_core(away_own)
    made = [(blocks, active, grad_hidden)]
    chips = [to_chip(owns[0])]
    sums = []
    for i in range(len(owns)):
        chip = chips[i]
        if i + 1 < len(owns):
            own, chip = barrier((owns[i + 1], chip))
            chips.append(to_chip(own))
        if i:
            chip, away, back_own = barrier((chip, away, back_own))
            sums.append(reduce_core(away, near))
        far = to_core(chip)
        active, grad_hidden, away, near = expert_step([far, chip], w_in, w_out)
        made.append(([far, chip], active, grad_hidden))
    away, sums[-1] = barrier((away, sums[-1]))
    sums.append(reduce_core(away, near))
    returned = kernel_call(
        functools.partial(return_kernel, capacity), shape(columns * width // LANES, LANES), SMALL, 10**6, 10**6
    )(near_own, back_own, *sums)
    arrived = exchange(returned, experts).reshape(columns, width)
    grad_in, grad_out = weight_grads(made, *w_in.shape)
    first, second = places(ids, slots, capacity, columns)
    place = (first | second).astype(BF)
    token_grad = dot(place, arrived, ((0,), (0,))).astype(BF)
    return token_grad, grad_in[None], grad_out[None]


def solution(mesh):
    rows = P(("expert", "replica"), None)
    return jax.shard_map(
        shards,
        mesh=mesh,
        in_specs=(rows, rows, rows, rows, rows, P("expert", None, "replica"), P("expert", "replica", None)),
        out_specs=(rows, P("expert", None, "replica"), P("expert", "replica", None)),
        check_vma=False,
    )
```

```python
import functools

import jax
import jax.numpy as jnp
from jax import lax
from jax.experimental import pallas as pl
from jax.experimental.pallas import tpu as pltpu
from jax.sharding import PartitionSpec as P

BF = jnp.bfloat16
F32 = jnp.float32
LANES = 128
SCALE = 0.7978845608
CUBE = 0.044715
TO_CORE = ((0, 1), (1, 0), (2, 3), (3, 2))
TO_CHIP = ((0, 2), (2, 0), (1, 3), (3, 1))
SPLIT = (32, 32)
SMALL = 16 * 2**20
LARGE = 56 * 2**20
EXPERT = 24 * 2**20
GRADS = 56 * 2**20


def dot(a, b, dims):
    return lax.dot_general(a, b, ((dims[0], dims[1]), ((), ())), preferred_element_type=F32)


def kernel_call(body, out_shape, limit, flops, size, **kw):
    return pl.pallas_call(
        body,
        out_shape=out_shape,
        compiler_params=pltpu.CompilerParams(vmem_limit_bytes=limit),
        cost_estimate=pl.CostEstimate(flops=flops, bytes_accessed=size, transcendentals=0),
        **kw,
    )


def shape(rows, width, dtype=BF):
    return jax.ShapeDtypeStruct((rows, width), dtype)


def to_core(rows):
    return lax.ppermute(rows, "replica", TO_CORE)


def to_chip(rows):
    return lax.ppermute(rows, "replica", TO_CHIP)


def places(ids, slots, capacity, columns):
    target = jnp.where(slots >= 0, ids * capacity + slots, -1)
    column_ids = lax.broadcasted_iota(jnp.int32, (columns, target.shape[1]), 0)
    return column_ids == target[0:1, :], column_ids == target[1:2, :]


def pack(rows, experts):
    count, width = rows.shape
    return rows.reshape(count, width // LANES, LANES).reshape(experts, -1, LANES)


def dispatch_kernel(experts, capacity, tokens, upstream, ids, slots, gates, sent):
    columns = experts * capacity
    first, second = places(ids[...], slots[...], capacity, columns)
    place = jnp.where(first | second, 1.0, 0.0).astype(BF)
    gate = jnp.where(first, gates[0:1, :], 0.0) + jnp.where(second, gates[1:2, :], 0.0)
    slot_gate = jnp.sum(gate, axis=1, keepdims=True)
    rows = dot(place, tokens[...], ((1,), (0,)))
    grads = slot_gate * dot(place, upstream[...], ((1,), (0,)))
    both = jnp.concatenate([pack(rows, experts), pack(grads, experts)], axis=1)
    sent[...] = both.reshape(-1, LANES).astype(BF)


def unpack_kernel(start, senders, got, own):
    per = own.shape[0] * own.shape[1] // (senders * LANES)
    rows = got[pl.ds(start * per, senders * per), :]
    blocks = rows.astype(F32).reshape(senders, -1, LANES)
    per = blocks.shape[1] // 2
    n = own.shape[0] // 2
    own[pl.ds(0, n), :] = blocks[:, :per].reshape(n, -1).astype(BF)
    own[pl.ds(n, n), :] = blocks[:, per:].reshape(n, -1).astype(BF)


def expert_kernel(sizes, *refs):
    blocks, refs = refs[: len(sizes)], refs[len(sizes) :]
    w_in, w_out, active, grad_hidden, away, near = refs
    split = away.shape[0]
    x = jnp.concatenate([block[pl.ds(0, n), :] for n, block in zip(sizes, blocks)], axis=0)
    g = jnp.concatenate([block[pl.ds(n, n), :] for n, block in zip(sizes, blocks)], axis=0)
    hidden = dot(x, w_in[...], ((1,), (0,)))
    carried = dot(g, w_out[...], ((1,), (1,)))
    square = hidden * hidden
    bend = jnp.tanh(hidden * (SCALE + SCALE * CUBE * square))
    lift = 0.5 * (1.0 + bend)
    active[...] = (hidden * lift).astype(BF)
    slope = lift + hidden * (1.0 - bend * bend) * (0.5 * SCALE + 1.5 * SCALE * CUBE * square)
    back = (slope * carried).astype(BF)
    grad_hidden[...] = back
    part = dot(back, w_in[...], ((1,), (1,)))
    away[...] = part[:split].astype(BF)
    near[...] = part[split:]


def expert_step(blocks, w_in, w_out):
    width, units = w_in.shape
    sizes = [block.shape[0] // 2 for block in blocks]
    rows = sum(sizes)
    return kernel_call(
        functools.partial(expert_kernel, sizes),
        [shape(rows, units), shape(rows, units), shape(rows // 2, width), shape(rows // 2, width, F32)],
        EXPERT,
        6 * rows * width * units,
        4 * width * units + 14 * rows * width,
    )(*blocks, w_in, w_out)


def weight_grads_kernel(sizes, runs, *refs):
    blocks, refs = refs[: len(sizes)], refs[len(sizes) :]
    count = len(runs)
    actives, refs = refs[:count], refs[count:]
    grad_hiddens, (grad_in, grad_out) = refs[:count], refs[count:]
    out_sum = in_sum = None
    at = 0
    for active, grad_hidden, run in zip(actives, grad_hiddens, runs):
        sides = list(zip(sizes[at : at + run], blocks[at : at + run]))
        at += run
        x = jnp.concatenate([block[pl.ds(0, n), :] for n, block in sides], axis=0)
        g = jnp.concatenate([block[pl.ds(n, n), :] for n, block in sides], axis=0)
        out_part = dot(active[...], g, ((0,), (0,)))
        in_part = dot(grad_hidden[...], x, ((0,), (0,)))
        out_sum = out_part if out_sum is None else out_sum + out_part
        in_sum = in_part if in_sum is None else in_sum + in_part
    grad_out[...] = out_sum.astype(BF)
    grad_in[...] = in_sum.T.astype(BF)


def weight_grads(made, width, units):
    tile = 256
    blocks = [block for group, _, _ in made for block in group]
    sizes = [block.shape[0] // 2 for block in blocks]
    runs = [len(group) for group, _, _ in made]
    rows = [active.shape[0] for _, active, _ in made]
    columns = [pl.BlockSpec((n, tile), lambda j: (0, j)) for n in rows]
    return kernel_call(
        functools.partial(weight_grads_kernel, sizes, runs),
        [shape(width, units), shape(units, width)],
        GRADS,
        4 * sum(rows) * width * units,
        4 * width * units + 8 * sum(rows) * width,
        grid=(units // tile,),
        in_specs=[pl.BlockSpec((2 * n, width), lambda j: (0, 0)) for n in sizes] + columns + columns,
        out_specs=[pl.BlockSpec((width, tile), lambda j: (0, j)), pl.BlockSpec((tile, width), lambda j: (j, 0))],
    )(*blocks, *[m[1] for m in made], *[m[2] for m in made])


def first_return_kernel(capacity, near, back, chip, packed, base):
    n = chip.shape[0]
    rows = near[pl.ds(0, n), :] + back[pl.ds(0, n), :].astype(F32) + chip[...].astype(F32)
    packed[...] = pack(rows, n // capacity).reshape(-1, LANES).astype(BF)
    rest = pl.ds(n, near.shape[0] - n)
    base[...] = near[rest, :] + back[rest, :].astype(F32)


def last_return_kernel(capacity, packed, base, chip, out):
    done = packed.shape[0]
    out[pl.ds(0, done), :] = packed[...]
    rows = base[...] + chip[...].astype(F32)
    out[pl.ds(done, out.shape[0] - done), :] = pack(rows, rows.shape[0] // capacity).reshape(-1, LANES).astype(BF)


def exchange(blocks, experts):
    moved = lax.all_to_all(blocks.reshape(experts, -1, LANES), "expert", split_axis=0, concat_axis=0, tiled=True)
    return moved.reshape(-1, LANES)


def shards(tokens, upstream, expert_ids, slot_index, gate_weights, in_weight, out_weight):
    token_count, width = tokens.shape
    experts = lax.axis_size("expert")
    capacity = 5 * token_count // (2 * experts)
    columns = experts * capacity
    per = width // LANES * capacity * 2
    ids, slots, gates = expert_ids.T, slot_index.T, gate_weights.T
    sent = kernel_call(
        functools.partial(dispatch_kernel, experts, capacity), shape(experts * per, LANES), LARGE, 1, 1
    )(tokens, upstream, ids, slots, gates)
    got = exchange(sent, experts)
    w_in = in_weight[0]
    w_out = out_weight[0]
    owns = []
    start = 0
    for senders in SPLIT:
        owns.append(
            kernel_call(
                functools.partial(unpack_kernel, start, senders),
                shape(2 * senders * capacity, width),
                SMALL,
                10**6,
                10**6,
            )(got)
        )
        start += senders
    barrier = lax.optimization_barrier
    chips = [to_chip(own) for own in owns]
    cores = [to_core(own) for own in owns]
    blocks = cores + owns
    chips[0], blocks[0], blocks[1] = barrier((chips[0], blocks[0], blocks[1]))
    active, grad_hidden, away_own, near_own = expert_step(blocks, w_in, w_out)
    back_own = to_core(away_own)
    made = [(blocks, active, grad_hidden)]
    sums = []
    for i, chip in enumerate(chips):
        if i:
            chip, sent, back_own = barrier((chip, sent, back_own))
            sums.append(to_chip(sent))
        far = to_core(chip)
        active, grad_hidden, away, near = expert_step([far, chip], w_in, w_out)
        made.append(([far, chip], active, grad_hidden))
        if sums:
            near, sums[-1] = barrier((near, sums[-1]))
        sent = (near + to_core(away).astype(F32)).astype(BF)
    sums.append(to_chip(sent))
    per = width // LANES
    n = sums[0].shape[0]
    packed, base = kernel_call(
        functools.partial(first_return_kernel, capacity),
        [shape(n * per, LANES), shape(columns - n, width, F32)],
        SMALL,
        10**6,
        10**6,
    )(near_own, back_own, sums[0])
    returned = kernel_call(
        functools.partial(last_return_kernel, capacity), shape(columns * per, LANES), SMALL, 10**6, 10**6
    )(packed, base, sums[1])
    arrived = exchange(returned, experts).reshape(columns, width)
    grad_in, grad_out = weight_grads(made, *w_in.shape)
    first, second = places(ids, slots, capacity, columns)
    place = (first | second).astype(BF)
    token_grad = dot(place, arrived, ((0,), (0,))).astype(BF)
    return token_grad, grad_in[None], grad_out[None]


def solution(mesh):
    rows = P(("expert", "replica"), None)
    return jax.shard_map(
        shards,
        mesh=mesh,
        in_specs=(rows, rows, rows, rows, rows, P("expert", None, "replica"), P("expert", "replica", None)),
        out_specs=(rows, P("expert", None, "replica"), P("expert", "replica", None)),
        check_vma=False,
    )
```

```python
import functools

import jax
import jax.numpy as jnp
from jax import lax
from jax.experimental import pallas as pl
from jax.experimental.pallas import tpu as pltpu
from jax.sharding import PartitionSpec as P

BF = jnp.bfloat16
F32 = jnp.float32
LANES = 128
SCALE = 0.7978845608
CUBE = 0.044715
TO_CORE = ((0, 1), (1, 0), (2, 3), (3, 2))
TO_CHIP = ((0, 2), (2, 0), (1, 3), (3, 1))
SPLIT = (32, 32)
FAR = 4
BACK = 2
SMALL = 16 * 2**20
LARGE = 56 * 2**20
EXPERT = 24 * 2**20
GRADS = 56 * 2**20


def dot(a, b, dims):
    return lax.dot_general(a, b, ((dims[0], dims[1]), ((), ())), preferred_element_type=F32)


def kernel_call(body, out_shape, limit, flops, size, **kw):
    return pl.pallas_call(
        body,
        out_shape=out_shape,
        compiler_params=pltpu.CompilerParams(vmem_limit_bytes=limit),
        cost_estimate=pl.CostEstimate(flops=flops, bytes_accessed=size, transcendentals=0),
        **kw,
    )


def shape(rows, width, dtype=BF):
    return jax.ShapeDtypeStruct((rows, width), dtype)


def to_core(rows):
    return lax.ppermute(rows, "replica", TO_CORE)


def to_chip(rows):
    return lax.ppermute(rows, "replica", TO_CHIP)


def places(ids, slots, capacity, columns):
    target = jnp.where(slots >= 0, ids * capacity + slots, -1)
    column_ids = lax.broadcasted_iota(jnp.int32, (columns, target.shape[1]), 0)
    return column_ids == target[0:1, :], column_ids == target[1:2, :]


def pack(rows, experts):
    count, width = rows.shape
    return rows.reshape(count, width // LANES, LANES).reshape(experts, -1, LANES)


def dispatch_kernel(experts, capacity, tokens, upstream, ids, slots, gates, sent):
    columns = experts * capacity
    first, second = places(ids[...], slots[...], capacity, columns)
    place = jnp.where(first | second, 1.0, 0.0).astype(BF)
    gate = jnp.where(first, gates[0:1, :], 0.0) + jnp.where(second, gates[1:2, :], 0.0)
    slot_gate = jnp.sum(gate, axis=1, keepdims=True)
    rows = dot(place, tokens[...], ((1,), (0,)))
    grads = slot_gate * dot(place, upstream[...], ((1,), (0,)))
    both = jnp.concatenate([pack(rows, experts), pack(grads, experts)], axis=1)
    sent[...] = both.reshape(-1, LANES).astype(BF)


def unpack_kernel(start, senders, got, own):
    per = own.shape[0] * own.shape[1] // (senders * LANES)
    rows = got[pl.ds(start * per, senders * per), :]
    blocks = rows.astype(F32).reshape(senders, -1, LANES)
    per = blocks.shape[1] // 2
    n = own.shape[0] // 2
    own[pl.ds(0, n), :] = blocks[:, :per].reshape(n, -1).astype(BF)
    own[pl.ds(n, n), :] = blocks[:, per:].reshape(n, -1).astype(BF)


def rows_of(counts, refs):
    x, g = [], []
    at = 0
    for count in counts:
        pieces = refs[at : at + count]
        at += count
        if count == 1:
            n = pieces[0].shape[0] // 2
            x.append(pieces[0][pl.ds(0, n), :])
            g.append(pieces[0][pl.ds(n, n), :])
        else:
            x += [piece[...] for piece in pieces[: count // 2]]
            g += [piece[...] for piece in pieces[count // 2 :]]
    return jnp.concatenate(x, axis=0), jnp.concatenate(g, axis=0)


def expert_kernel(counts, *refs):
    blocks, refs = refs[: sum(counts)], refs[sum(counts) :]
    w_in, w_out, active, grad_hidden, away, near = refs
    split = away.shape[0]
    x, g = rows_of(counts, blocks)
    hidden = dot(x, w_in[...], ((1,), (0,)))
    carried = dot(g, w_out[...], ((1,), (1,)))
    square = hidden * hidden
    bend = jnp.tanh(hidden * (SCALE + SCALE * CUBE * square))
    lift = 0.5 * (1.0 + bend)
    active[...] = (hidden * lift).astype(BF)
    slope = lift + hidden * (1.0 - bend * bend) * (0.5 * SCALE + 1.5 * SCALE * CUBE * square)
    back = (slope * carried).astype(BF)
    grad_hidden[...] = back
    part = dot(back, w_in[...], ((1,), (1,)))
    away[...] = part[:split].astype(BF)
    near[...] = part[split:]


def expert_step(blocks, w_in, w_out):
    width, units = w_in.shape
    counts = [len(block) for block in blocks]
    blocks = [piece for block in blocks for piece in block]
    rows = sum(piece.shape[0] for piece in blocks) // 2
    return kernel_call(
        functools.partial(expert_kernel, counts),
        [shape(rows, units), shape(rows, units), shape(rows // 2, width), shape(rows // 2, width, F32)],
        EXPERT,
        6 * rows * width * units,
        4 * width * units + 14 * rows * width,
    )(*blocks, w_in, w_out)


def weight_grads_kernel(groups, *refs):
    total = sum(sum(counts) for counts in groups)
    blocks, refs = refs[:total], refs[total:]
    actives, refs = refs[: len(groups)], refs[len(groups) :]
    grad_hiddens, (grad_in, grad_out) = refs[: len(groups)], refs[len(groups) :]
    out_sum = in_sum = None
    at = 0
    for active, grad_hidden, counts in zip(actives, grad_hiddens, groups):
        x, g = rows_of(counts, blocks[at : at + sum(counts)])
        at += sum(counts)
        out_part = dot(active[...], g, ((0,), (0,)))
        in_part = dot(grad_hidden[...], x, ((0,), (0,)))
        out_sum = out_part if out_sum is None else out_sum + out_part
        in_sum = in_part if in_sum is None else in_sum + in_part
    grad_out[...] = out_sum.astype(BF)
    grad_in[...] = in_sum.T.astype(BF)


def weight_grads(made, width, units):
    tile = 256
    groups = [[len(block) for block in blocks] for blocks, _, _ in made]
    pieces = [piece for blocks, _, _ in made for block in blocks for piece in block]
    rows = [active.shape[0] for _, active, _ in made]
    columns = [pl.BlockSpec((n, tile), lambda j: (0, j)) for n in rows]
    return kernel_call(
        functools.partial(weight_grads_kernel, groups),
        [shape(width, units), shape(units, width)],
        GRADS,
        4 * sum(rows) * width * units,
        4 * width * units + 8 * sum(rows) * width,
        grid=(units // tile,),
        in_specs=[pl.BlockSpec(piece.shape, lambda j: (0, 0)) for piece in pieces] + columns + columns,
        out_specs=[pl.BlockSpec((width, tile), lambda j: (0, j)), pl.BlockSpec((tile, width), lambda j: (j, 0))],
    )(*pieces, *[m[1] for m in made], *[m[2] for m in made])


def core_pieces(rows, count):
    step = rows.shape[0] // count
    return [to_core(rows[i * step : (i + 1) * step]) for i in range(count)]


def first_return_kernel(capacity, near, back, chip, packed, base):
    n = chip.shape[0]
    rows = near[pl.ds(0, n), :] + back[pl.ds(0, n), :].astype(F32) + chip[...].astype(F32)
    packed[...] = pack(rows, n // capacity).reshape(-1, LANES).astype(BF)
    rest = pl.ds(n, near.shape[0] - n)
    base[...] = near[rest, :] + back[rest, :].astype(F32)


def last_return_kernel(capacity, packed, base, chip, out):
    done = packed.shape[0]
    out[pl.ds(0, done), :] = packed[...]
    rows = base[...] + chip[...].astype(F32)
    out[pl.ds(done, out.shape[0] - done), :] = pack(rows, rows.shape[0] // capacity).reshape(-1, LANES).astype(BF)


def exchange(blocks, experts):
    moved = lax.all_to_all(blocks.reshape(experts, -1, LANES), "expert", split_axis=0, concat_axis=0, tiled=True)
    return moved.reshape(-1, LANES)


def shards(tokens, upstream, expert_ids, slot_index, gate_weights, in_weight, out_weight):
    token_count, width = tokens.shape
    experts = lax.axis_size("expert")
    capacity = 5 * token_count // (2 * experts)
    columns = experts * capacity
    per = width // LANES * capacity * 2
    ids, slots, gates = expert_ids.T, slot_index.T, gate_weights.T
    sent = kernel_call(
        functools.partial(dispatch_kernel, experts, capacity), shape(experts * per, LANES), LARGE, 1, 1
    )(tokens, upstream, ids, slots, gates)
    got = exchange(sent, experts)
    w_in = in_weight[0]
    w_out = out_weight[0]
    owns = []
    start = 0
    for senders in SPLIT:
        owns.append(
            kernel_call(
                functools.partial(unpack_kernel, start, senders),
                shape(2 * senders * capacity, width),
                SMALL,
                10**6,
                10**6,
            )(got)
        )
        start += senders
    barrier = lax.optimization_barrier
    chips = [to_chip(own) for own in owns]
    cores = [to_core(own) for own in owns]
    blocks = [[block] for block in cores + owns]
    active, grad_hidden, away_own, near_own = expert_step(blocks, w_in, w_out)
    back_own = to_core(away_own)
    made = [(blocks, active, grad_hidden)]
    sums = []
    for i, chip in enumerate(chips):
        if i:
            chip, sent, back_own = barrier((chip, sent, back_own))
            sums.append(to_chip(sent))
        blocks = [core_pieces(chip, FAR), [chip]]
        active, grad_hidden, away, near = expert_step(blocks, w_in, w_out)
        made.append((blocks, active, grad_hidden))
        if sums:
            near, sums[-1] = barrier((near, sums[-1]))
        sent = (near + jnp.concatenate(core_pieces(away, BACK), axis=0).astype(F32)).astype(BF)
    sums.append(to_chip(sent))
    per = width // LANES
    n = sums[0].shape[0]
    packed, base = kernel_call(
        functools.partial(first_return_kernel, capacity),
        [shape(n * per, LANES), shape(columns - n, width, F32)],
        SMALL,
        10**6,
        10**6,
    )(near_own, back_own, sums[0])
    returned = kernel_call(
        functools.partial(last_return_kernel, capacity), shape(columns * per, LANES), SMALL, 10**6, 10**6
    )(packed, base, sums[1])
    arrived = exchange(returned, experts).reshape(columns, width)
    grad_in, grad_out = weight_grads(made, *w_in.shape)
    first, second = places(ids, slots, capacity, columns)
    place = (first | second).astype(BF)
    token_grad = dot(place, arrived, ((0,), (0,))).astype(BF)
    return token_grad, grad_in[None], grad_out[None]


def solution(mesh):
    rows = P(("expert", "replica"), None)
    return jax.shard_map(
        shards,
        mesh=mesh,
        in_specs=(rows, rows, rows, rows, rows, P("expert", None, "replica"), P("expert", "replica", None)),
        out_specs=(rows, P("expert", None, "replica"), P("expert", "replica", None)),
        check_vma=False,
    )
```

```python
import functools

import jax
import jax.numpy as jnp
from jax import lax
from jax.experimental import pallas as pl
from jax.experimental.pallas import tpu as pltpu
from jax.sharding import PartitionSpec as P

BF = jnp.bfloat16
F32 = jnp.float32
LANES = 128
SCALE = 0.7978845608
CUBE = 0.044715
TO_CORE = ((0, 1), (1, 0), (2, 3), (3, 2))
TO_CHIP = ((0, 2), (2, 0), (1, 3), (3, 1))
SPLIT = (32, 32)
FAR = (4, 1)
BACK = (2, 2)
SMALL = 16 * 2**20
LARGE = 56 * 2**20
EXPERT = 24 * 2**20
GRADS = 56 * 2**20


def dot(a, b, dims):
    return lax.dot_general(a, b, ((dims[0], dims[1]), ((), ())), preferred_element_type=F32)


def kernel_call(body, out_shape, limit, flops, size, **kw):
    return pl.pallas_call(
        body,
        out_shape=out_shape,
        compiler_params=pltpu.CompilerParams(vmem_limit_bytes=limit),
        cost_estimate=pl.CostEstimate(flops=flops, bytes_accessed=size, transcendentals=0),
        **kw,
    )


def shape(rows, width, dtype=BF):
    return jax.ShapeDtypeStruct((rows, width), dtype)


def to_core(rows):
    return lax.ppermute(rows, "replica", TO_CORE)


def to_chip(rows):
    return lax.ppermute(rows, "replica", TO_CHIP)


def places(ids, slots, capacity, columns):
    target = jnp.where(slots >= 0, ids * capacity + slots, -1)
    column_ids = lax.broadcasted_iota(jnp.int32, (columns, target.shape[1]), 0)
    return column_ids == target[0:1, :], column_ids == target[1:2, :]


def pack(rows, experts):
    count, width = rows.shape
    return rows.reshape(count, width // LANES, LANES).reshape(experts, -1, LANES)


def dispatch_kernel(experts, capacity, tokens, upstream, ids, slots, gates, sent):
    columns = experts * capacity
    first, second = places(ids[...], slots[...], capacity, columns)
    place = jnp.where(first | second, 1.0, 0.0).astype(BF)
    gate = jnp.where(first, gates[0:1, :], 0.0) + jnp.where(second, gates[1:2, :], 0.0)
    slot_gate = jnp.sum(gate, axis=1, keepdims=True)
    rows = dot(place, tokens[...], ((1,), (0,)))
    grads = slot_gate * dot(place, upstream[...], ((1,), (0,)))
    both = jnp.concatenate([pack(rows, experts), pack(grads, experts)], axis=1)
    sent[...] = both.reshape(-1, LANES).astype(BF)


def unpack_kernel(start, senders, got, own):
    per = own.shape[0] * own.shape[1] // (senders * LANES)
    rows = got[pl.ds(start * per, senders * per), :]
    blocks = rows.astype(F32).reshape(senders, -1, LANES)
    per = blocks.shape[1] // 2
    n = own.shape[0] // 2
    own[pl.ds(0, n), :] = blocks[:, :per].reshape(n, -1).astype(BF)
    own[pl.ds(n, n), :] = blocks[:, per:].reshape(n, -1).astype(BF)


def rows_of(counts, refs):
    x, g = [], []
    at = 0
    for count in counts:
        pieces = refs[at : at + count]
        at += count
        if count == 1:
            n = pieces[0].shape[0] // 2
            x.append(pieces[0][pl.ds(0, n), :])
            g.append(pieces[0][pl.ds(n, n), :])
        else:
            x += [piece[...] for piece in pieces[: count // 2]]
            g += [piece[...] for piece in pieces[count // 2 :]]
    return jnp.concatenate(x, axis=0), jnp.concatenate(g, axis=0)


def expert_kernel(counts, *refs):
    blocks, refs = refs[: sum(counts)], refs[sum(counts) :]
    w_in, w_out, active, grad_hidden, away, near = refs
    split = away.shape[0]
    x, g = rows_of(counts, blocks)
    hidden = dot(x, w_in[...], ((1,), (0,)))
    carried = dot(g, w_out[...], ((1,), (1,)))
    square = hidden * hidden
    bend = jnp.tanh(hidden * (SCALE + SCALE * CUBE * square))
    lift = 0.5 * (1.0 + bend)
    active[...] = (hidden * lift).astype(BF)
    slope = lift + hidden * (1.0 - bend * bend) * (0.5 * SCALE + 1.5 * SCALE * CUBE * square)
    back = (slope * carried).astype(BF)
    grad_hidden[...] = back
    part = dot(back, w_in[...], ((1,), (1,)))
    away[...] = part[:split].astype(BF)
    near[...] = part[split:]


def expert_step(blocks, w_in, w_out):
    width, units = w_in.shape
    counts = [len(block) for block in blocks]
    blocks = [piece for block in blocks for piece in block]
    rows = sum(piece.shape[0] for piece in blocks) // 2
    return kernel_call(
        functools.partial(expert_kernel, counts),
        [shape(rows, units), shape(rows, units), shape(rows // 2, width), shape(rows // 2, width, F32)],
        EXPERT,
        6 * rows * width * units,
        4 * width * units + 14 * rows * width,
    )(*blocks, w_in, w_out)


def weight_grads_kernel(groups, *refs):
    total = sum(sum(counts) for counts in groups)
    blocks, refs = refs[:total], refs[total:]
    actives, refs = refs[: len(groups)], refs[len(groups) :]
    grad_hiddens, (grad_in, grad_out) = refs[: len(groups)], refs[len(groups) :]
    out_sum = in_sum = None
    at = 0
    for active, grad_hidden, counts in zip(actives, grad_hiddens, groups):
        x, g = rows_of(counts, blocks[at : at + sum(counts)])
        at += sum(counts)
        out_part = dot(active[...], g, ((0,), (0,)))
        in_part = dot(grad_hidden[...], x, ((0,), (0,)))
        out_sum = out_part if out_sum is None else out_sum + out_part
        in_sum = in_part if in_sum is None else in_sum + in_part
    grad_out[...] = out_sum.astype(BF)
    grad_in[...] = in_sum.T.astype(BF)


def weight_grads(made, width, units):
    tile = 256
    groups = [[len(block) for block in blocks] for blocks, _, _ in made]
    pieces = [piece for blocks, _, _ in made for block in blocks for piece in block]
    rows = [active.shape[0] for _, active, _ in made]
    columns = [pl.BlockSpec((n, tile), lambda j: (0, j)) for n in rows]
    return kernel_call(
        functools.partial(weight_grads_kernel, groups),
        [shape(width, units), shape(units, width)],
        GRADS,
        4 * sum(rows) * width * units,
        4 * width * units + 8 * sum(rows) * width,
        grid=(units // tile,),
        in_specs=[pl.BlockSpec(piece.shape, lambda j: (0, 0)) for piece in pieces] + columns + columns,
        out_specs=[pl.BlockSpec((width, tile), lambda j: (0, j)), pl.BlockSpec((tile, width), lambda j: (j, 0))],
    )(*pieces, *[m[1] for m in made], *[m[2] for m in made])


def core_pieces(rows, count):
    step = rows.shape[0] // count
    return [to_core(rows[i * step : (i + 1) * step]) for i in range(count)]


def first_return_kernel(capacity, near, back, chip, packed, base):
    n = chip.shape[0]
    rows = near[pl.ds(0, n), :] + back[pl.ds(0, n), :].astype(F32) + chip[...].astype(F32)
    packed[...] = pack(rows, n // capacity).reshape(-1, LANES).astype(BF)
    rest = pl.ds(n, near.shape[0] - n)
    rows = near[rest, :] + back[rest, :].astype(F32)
    base[...] = pack(rows, rows.shape[0] // capacity).reshape(-1, LANES)


def last_return_kernel(packed, base, chip, out):
    done = packed.shape[0]
    out[pl.ds(0, done), :] = packed[...]
    out[pl.ds(done, out.shape[0] - done), :] = (base[...] + chip[...].astype(F32)).astype(BF)


def sum_kernel(capacity, near, *refs):
    backs, sent = refs[:-1], refs[-1]
    n = near.shape[0]
    rows = near[...] + jnp.concatenate([v[...] for v in backs], axis=0).astype(F32)
    sent[...] = pack(rows, n // capacity).reshape(-1, LANES).astype(BF)


def combine_kernel(experts, capacity, arrived, ids, slots, out):
    columns = experts * capacity
    rows = arrived[...].astype(F32).reshape(columns, -1).astype(BF)
    first, second = places(ids[...], slots[...], capacity, columns)
    place = jnp.where(first | second, 1.0, 0.0).astype(BF)
    out[...] = dot(place, rows, ((0,), (0,))).astype(BF)


def exchange(blocks, experts):
    moved = lax.all_to_all(blocks.reshape(experts, -1, LANES), "expert", split_axis=0, concat_axis=0, tiled=True)
    return moved.reshape(-1, LANES)


def shards(tokens, upstream, expert_ids, slot_index, gate_weights, in_weight, out_weight):
    token_count, width = tokens.shape
    experts = lax.axis_size("expert")
    capacity = 5 * token_count // (2 * experts)
    columns = experts * capacity
    per = width // LANES * capacity * 2
    ids, slots, gates = expert_ids.T, slot_index.T, gate_weights.T
    sent = kernel_call(
        functools.partial(dispatch_kernel, experts, capacity), shape(experts * per, LANES), LARGE, 1, 1
    )(tokens, upstream, ids, slots, gates)
    got = exchange(sent, experts)
    w_in = in_weight[0]
    w_out = out_weight[0]
    owns = []
    start = 0
    for senders in SPLIT:
        owns.append(
            kernel_call(
                functools.partial(unpack_kernel, start, senders),
                shape(2 * senders * capacity, width),
                SMALL,
                10**6,
                10**6,
            )(got)
        )
        start += senders
    barrier = lax.optimization_barrier
    chips = [to_chip(own) for own in owns]
    cores = [to_core(own) for own in owns]
    blocks = [[block] for block in cores + owns]
    active, grad_hidden, away_own, near_own = expert_step(blocks, w_in, w_out)
    back_own = to_core(away_own)
    made = [(blocks, active, grad_hidden)]
    sums = []
    for i, chip in enumerate(chips):
        if i:
            chip, sent, back_own = barrier((chip, sent, back_own))
            sums.append(to_chip(sent))
        blocks = [core_pieces(chip, FAR[i]), [chip]]
        active, grad_hidden, away, near = expert_step(blocks, w_in, w_out)
        made.append((blocks, active, grad_hidden))
        backs = core_pieces(away, BACK[i])
        if not sums:
            sent = (near + jnp.concatenate(backs, axis=0).astype(F32)).astype(BF)
    per = width // LANES
    n = sums[0].shape[0]
    rest = columns - n
    sent = kernel_call(
        functools.partial(sum_kernel, capacity), shape(rest * per, LANES), SMALL, 10**6, 10**6
    )(near, *backs)
    sent, sums[0] = barrier((sent, sums[0]))
    sums.append(to_chip(sent))
    packed, base = kernel_call(
        functools.partial(first_return_kernel, capacity),
        [shape(n * per, LANES), shape(rest * per, LANES, F32)],
        SMALL,
        10**6,
        10**6,
    )(near_own, back_own, sums[0])
    returned = kernel_call(
        last_return_kernel, shape(columns * per, LANES), SMALL, 10**6, 10**6
    )(packed, base, sums[1])
    arrived = exchange(returned, experts)
    grad_in, grad_out = weight_grads(made, *w_in.shape)
    token_grad = kernel_call(
        functools.partial(combine_kernel, experts, capacity), shape(token_count, width), SMALL, 10**6, 10**6
    )(arrived, ids, slots)
    return token_grad, grad_in[None], grad_out[None]


def solution(mesh):
    rows = P(("expert", "replica"), None)
    return jax.shard_map(
        shards,
        mesh=mesh,
        in_specs=(rows, rows, rows, rows, rows, P("expert", None, "replica"), P("expert", "replica", None)),
        out_specs=(rows, P("expert", None, "replica"), P("expert", "replica", None)),
        check_vma=False,
    )
```

```python
import functools

import jax
import jax.numpy as jnp
from jax import lax
from jax.experimental import pallas as pl
from jax.experimental.pallas import tpu as pltpu
from jax.sharding import PartitionSpec as P

BF = jnp.bfloat16
F32 = jnp.float32
LANES = 128
SCALE = 0.7978845608
CUBE = 0.044715
TO_CORE = ((0, 1), (1, 0), (2, 3), (3, 2))
TO_CHIP = ((0, 2), (2, 0), (1, 3), (3, 1))
SPLIT = (32, 32)
FAR = (4, 1)
BACK = (2, 2)
SMALL = 16 * 2**20
LARGE = 56 * 2**20
EXPERT = 24 * 2**20
GRADS = 56 * 2**20


def dot(a, b, dims):
    return lax.dot_general(a, b, ((dims[0], dims[1]), ((), ())), preferred_element_type=F32)


def kernel_call(body, out_shape, limit, flops, size, **kw):
    return pl.pallas_call(
        body,
        out_shape=out_shape,
        compiler_params=pltpu.CompilerParams(vmem_limit_bytes=limit),
        cost_estimate=pl.CostEstimate(flops=flops, bytes_accessed=size, transcendentals=0),
        **kw,
    )


def shape(rows, width, dtype=BF):
    return jax.ShapeDtypeStruct((rows, width), dtype)


def to_core(rows):
    return lax.ppermute(rows, "replica", TO_CORE)


def to_chip(rows):
    return lax.ppermute(rows, "replica", TO_CHIP)


def places(ids, slots, capacity, columns):
    target = jnp.where(slots >= 0, ids * capacity + slots, -1)
    column_ids = lax.broadcasted_iota(jnp.int32, (columns, target.shape[1]), 0)
    return column_ids == target[0:1, :], column_ids == target[1:2, :]


def pack(rows, experts):
    count, width = rows.shape
    return rows.reshape(count, width // LANES, LANES).reshape(experts, -1, LANES)


def dispatch_kernel(experts, capacity, tokens, upstream, ids, slots, gates, sent):
    columns = experts * capacity
    first, second = places(ids[...], slots[...], capacity, columns)
    place = jnp.where(first | second, 1.0, 0.0).astype(BF)
    gate = jnp.where(first, gates[0:1, :], 0.0) + jnp.where(second, gates[1:2, :], 0.0)
    slot_gate = jnp.sum(gate, axis=1, keepdims=True)
    rows = dot(place, tokens[...], ((1,), (0,)))
    grads = slot_gate * dot(place, upstream[...], ((1,), (0,)))
    both = jnp.concatenate([pack(rows, experts), pack(grads, experts)], axis=1)
    sent[...] = both.reshape(-1, LANES).astype(BF)


def unpack_kernel(start, senders, got, own):
    per = own.shape[0] * own.shape[1] // (senders * LANES)
    rows = got[pl.ds(start * per, senders * per), :]
    blocks = rows.astype(F32).reshape(senders, -1, LANES)
    per = blocks.shape[1] // 2
    n = own.shape[0] // 2
    own[pl.ds(0, n), :] = blocks[:, :per].reshape(n, -1).astype(BF)
    own[pl.ds(n, n), :] = blocks[:, per:].reshape(n, -1).astype(BF)


def rows_of(counts, refs):
    x, g = [], []
    at = 0
    for count in counts:
        pieces = refs[at : at + count]
        at += count
        if count == 1:
            n = pieces[0].shape[0] // 2
            x.append(pieces[0][pl.ds(0, n), :])
            g.append(pieces[0][pl.ds(n, n), :])
        else:
            x += [piece[...] for piece in pieces[: count // 2]]
            g += [piece[...] for piece in pieces[count // 2 :]]
    return jnp.concatenate(x, axis=0), jnp.concatenate(g, axis=0)


def expert_kernel(counts, *refs):
    blocks, refs = refs[: sum(counts)], refs[sum(counts) :]
    w_in, w_out, active, grad_hidden, away, near = refs
    split = away.shape[0]
    x, g = rows_of(counts, blocks)
    hidden = dot(x, w_in[...], ((1,), (0,)))
    carried = dot(g, w_out[...], ((1,), (1,)))
    square = hidden * hidden
    bend = jnp.tanh(hidden * (SCALE + SCALE * CUBE * square))
    lift = 0.5 * (1.0 + bend)
    active[...] = (hidden * lift).astype(BF)
    slope = lift + hidden * (1.0 - bend * bend) * (0.5 * SCALE + 1.5 * SCALE * CUBE * square)
    back = (slope * carried).astype(BF)
    grad_hidden[...] = back
    part = dot(back, w_in[...], ((1,), (1,)))
    away[...] = part[:split].astype(BF)
    near[...] = part[split:]


def expert_step(blocks, w_in, w_out):
    width, units = w_in.shape
    counts = [len(block) for block in blocks]
    blocks = [piece for block in blocks for piece in block]
    rows = sum(piece.shape[0] for piece in blocks) // 2
    return kernel_call(
        functools.partial(expert_kernel, counts),
        [shape(rows, units), shape(rows, units), shape(rows // 2, width), shape(rows // 2, width, F32)],
        EXPERT,
        6 * rows * width * units,
        4 * width * units + 14 * rows * width,
    )(*blocks, w_in, w_out)


def weight_grads_kernel(groups, *refs):
    total = sum(sum(counts) for counts in groups)
    blocks, refs = refs[:total], refs[total:]
    actives, refs = refs[: len(groups)], refs[len(groups) :]
    grad_hiddens, (grad_in, grad_out) = refs[: len(groups)], refs[len(groups) :]
    out_sum = in_sum = None
    at = 0
    for active, grad_hidden, counts in zip(actives, grad_hiddens, groups):
        x, g = rows_of(counts, blocks[at : at + sum(counts)])
        at += sum(counts)
        out_part = dot(active[...], g, ((0,), (0,)))
        in_part = dot(grad_hidden[...], x, ((0,), (0,)))
        out_sum = out_part if out_sum is None else out_sum + out_part
        in_sum = in_part if in_sum is None else in_sum + in_part
    grad_out[...] = out_sum.astype(BF)
    grad_in[...] = in_sum.T.astype(BF)


def weight_grads(made, width, units):
    tile = 256
    groups = [[len(block) for block in blocks] for blocks, _, _ in made]
    pieces = [piece for blocks, _, _ in made for block in blocks for piece in block]
    rows = [active.shape[0] for _, active, _ in made]
    columns = [pl.BlockSpec((n, tile), lambda j: (0, j)) for n in rows]
    return kernel_call(
        functools.partial(weight_grads_kernel, groups),
        [shape(width, units), shape(units, width)],
        GRADS,
        4 * sum(rows) * width * units,
        4 * width * units + 8 * sum(rows) * width,
        grid=(units // tile,),
        in_specs=[pl.BlockSpec(piece.shape, lambda j: (0, 0)) for piece in pieces] + columns + columns,
        out_specs=[pl.BlockSpec((width, tile), lambda j: (0, j)), pl.BlockSpec((tile, width), lambda j: (j, 0))],
    )(*pieces, *[m[1] for m in made], *[m[2] for m in made])


def core_pieces(rows, count):
    step = rows.shape[0] // count
    return [to_core(rows[i * step : (i + 1) * step]) for i in range(count)]


def first_return_kernel(capacity, near, back, chip, packed, base):
    n = chip.shape[0]
    rows = near[pl.ds(0, n), :] + back[pl.ds(0, n), :].astype(F32) + chip[...].astype(F32)
    packed[...] = pack(rows, n // capacity).reshape(-1, LANES).astype(BF)
    rest = pl.ds(n, near.shape[0] - n)
    base[...] = near[rest, :] + back[rest, :].astype(F32)


def last_return_kernel(capacity, packed, base, chip, out):
    done = packed.shape[0]
    out[pl.ds(0, done), :] = packed[...]
    rows = base[...] + chip[...].astype(F32)
    out[pl.ds(done, out.shape[0] - done), :] = pack(rows, rows.shape[0] // capacity).reshape(-1, LANES).astype(BF)


def exchange(blocks, experts):
    moved = lax.all_to_all(blocks.reshape(experts, -1, LANES), "expert", split_axis=0, concat_axis=0, tiled=True)
    return moved.reshape(-1, LANES)


def shards(tokens, upstream, expert_ids, slot_index, gate_weights, in_weight, out_weight):
    token_count, width = tokens.shape
    experts = lax.axis_size("expert")
    capacity = 5 * token_count // (2 * experts)
    columns = experts * capacity
    per = width // LANES * capacity * 2
    ids, slots, gates = expert_ids.T, slot_index.T, gate_weights.T
    sent = kernel_call(
        functools.partial(dispatch_kernel, experts, capacity), shape(experts * per, LANES), LARGE, 1, 1
    )(tokens, upstream, ids, slots, gates)
    got = exchange(sent, experts)
    w_in = in_weight[0]
    w_out = out_weight[0]
    owns = []
    start = 0
    for senders in SPLIT:
        owns.append(
            kernel_call(
                functools.partial(unpack_kernel, start, senders),
                shape(2 * senders * capacity, width),
                SMALL,
                10**6,
                10**6,
            )(got)
        )
        start += senders
    barrier = lax.optimization_barrier
    chips = [to_chip(own) for own in owns]
    cores = [to_core(own) for own in owns]
    blocks = [[block] for block in cores + owns]
    active, grad_hidden, away_own, near_own = expert_step(blocks, w_in, w_out)
    back_own = to_core(away_own)
    made = [(blocks, active, grad_hidden)]
    sums = []
    for i, chip in enumerate(chips):
        if i:
            chip, sent, back_own = barrier((chip, sent, back_own))
            sums.append(to_chip(sent))
        blocks = [core_pieces(chip, FAR[i]), [chip]]
        active, grad_hidden, away, near = expert_step(blocks, w_in, w_out)
        made.append((blocks, active, grad_hidden))
        if sums:
            near, sums[-1] = barrier((near, sums[-1]))
        sent = (near + jnp.concatenate(core_pieces(away, BACK[i]), axis=0).astype(F32)).astype(BF)
    sums.append(to_chip(sent))
    per = width // LANES
    n = sums[0].shape[0]
    packed, base = kernel_call(
        functools.partial(first_return_kernel, capacity),
        [shape(n * per, LANES), shape(columns - n, width, F32)],
        SMALL,
        10**6,
        10**6,
    )(near_own, back_own, sums[0])
    returned = kernel_call(
        functools.partial(last_return_kernel, capacity), shape(columns * per, LANES), SMALL, 10**6, 10**6
    )(packed, base, sums[1])
    arrived = exchange(returned, experts).reshape(columns, width)
    grad_in, grad_out = weight_grads(made, *w_in.shape)
    first, second = places(ids, slots, capacity, columns)
    place = (first | second).astype(BF)
    token_grad = dot(place, arrived, ((0,), (0,))).astype(BF)
    return token_grad, grad_in[None], grad_out[None]


def solution(mesh):
    rows = P(("expert", "replica"), None)
    return jax.shard_map(
        shards,
        mesh=mesh,
        in_specs=(rows, rows, rows, rows, rows, P("expert", None, "replica"), P("expert", "replica", None)),
        out_specs=(rows, P("expert", None, "replica"), P("expert", "replica", None)),
        check_vma=False,
    )
```
